32 devices in a mesh: anim: 8 (over y, x, core), snp: 4 (over z).
Axes of the slice: x: 2, y: 2, z: 4, core: 2. Of those that a mesh axis runs over, the one named last changes fastest.
Arguments:
- core_geno: bfloat16 [12288, 49152], P('anim', 'snp'), may hold values from -10 to 10, as said below
- noncore_geno: bfloat16 [6144, 49152], P('anim', 'snp'), may hold values from -10 to 10, as said below
- core_inv: bfloat16 [12288, 12288], P('anim', 'snp'), may hold values from -0.0546875 to 0.0546875
- snp_effects: bfloat16 [256, 49152], P(None, 'snp'), may hold values from -0.02734375 to 0.02734375
- noncore_scale: float32 [6144], P('anim'), may hold values from 0.5 to 2
Outputs:
- noncore_out: float32 [256, 6144], P(None, 'anim')
- core_out: float32 [256, 12288], P(None, ('anim', 'snp'))
The draws below stay inside these ranges and needn't reach their ends.
Inputs may be any that keep to these rules, and one draw needn't show every extreme that they name: `core_geno`: each column j is (c - 2 p_j) / sqrt(2 p_j (1 - p_j)) for codes c in 0, 1, 2 and a column frequency p_j shared with noncore_geno. `noncore_geno`: each column j is (c - 2 p_j) / sqrt(2 p_j (1 - p_j)) for codes c in 0, 1, 2 and a column frequency p_j shared with core_geno.
All inputs are finite; a program needn't handle non-finite values.
Results may differ from the reference program's by a relative error of at most 0.008.
Values may be sent and summed in bfloat16 or wider, within the bound.
No kernel may reach another device: no remote copies, remote signals or barrier semaphores. Data moves between devices by JAX's collectives and lax.ppermute only.
A program may use at most 128 MiB of HBM per device.

```python
import math
import jax
import jax.numpy as jnp
from jax import lax

NSNP = 49152
NCORE = 12288
REPS = 256
NNON = 6144


def genotype_rows(key, count, salt):
    lowest = 0.05
    freq = jax.random.uniform(jax.random.fold_in(key, 11), (NSNP,), jnp.float32, lowest, 0.5)
    spread = jnp.sqrt(2.0 * freq * (1.0 - freq))
    row_key = jax.random.fold_in(key, salt)

    def one_row(index):
        draws = jax.random.uniform(jax.random.fold_in(row_key, index), (2, NSNP), jnp.float32)
        codes = jnp.sum((draws < freq[None, :]).astype(jnp.float32), axis=0)
        return ((codes - 2.0 * freq) / spread).astype(jnp.bfloat16)
    return lax.map(one_row, jnp.arange(count, dtype=jnp.int32))


def draw_core_geno(key, part):
    return genotype_rows(key, NCORE, 23)


def draw_noncore_geno(key, part):
    return genotype_rows(key, NNON, 37)


def level_of(stream_key, shape, cuts, low, largest):
    gain, own = 1.0, jax.random.fold_in(stream_key, 6)
    for axis_at, blocks in cuts:
        heights = jnp.exp(jax.random.uniform(jax.random.fold_in(own, axis_at), (blocks,), jnp.float32, low / len(cuts), largest / len(cuts)))
        gain = gain * jnp.repeat(heights, shape[axis_at] // blocks).reshape([-1 if axis == axis_at else 1 for axis in range(len(shape))])
    return gain


def centred(rng, dims, deviation, bound, split=(), kind=jnp.bfloat16):
    entries = jax.random.normal(rng, dims, jnp.float32) * deviation
    if len(split) > 0:
        entries = level_of(rng, dims, split, -0.22, 0.18) * entries
    return jnp.clip(entries, min=-bound, max=bound).astype(kind)


def setup_inputs(seed: int = 0) -> dict:
    key_of = jax.random.split(jax.random.key(seed), 6)
    core_geno = draw_core_geno(jax.random.fold_in(key_of[5], 71), 0)
    noncore_geno = draw_noncore_geno(jax.random.fold_in(key_of[5], 71), 0)
    core_inv = centred(key_of[2], (NCORE, NCORE), NCORE ** -0.5, 0.0546875, ((0, 8), (1, 4)))
    snp_effects = centred(key_of[3], (REPS, NSNP), NSNP ** -0.5, 0.02734375, ((1, 4),))
    noncore_scale = jnp.clip(jnp.exp(math.log(2.0) - 1.3862944 * jax.random.uniform(key_of[4], (NNON,), jnp.float32) ** level_of(key_of[4], (NNON,), ((0, 8),), -0.2, 0.2)), 0.5, 2.0)
    return dict(core_geno=core_geno, noncore_geno=noncore_geno, core_inv=core_inv, snp_effects=snp_effects, noncore_scale=noncore_scale)


def reference(core_geno, noncore_geno, core_inv, snp_effects, noncore_scale):
    f32 = jnp.float32
    bf16 = jnp.bfloat16
    core_vals = jnp.dot(snp_effects, core_geno.T, preferred_element_type=f32).astype(bf16)
    noncore_vals = jnp.dot(snp_effects, noncore_geno.T, preferred_element_type=f32)
    core_weights = jnp.dot(core_vals, core_inv.T, preferred_element_type=f32).astype(bf16)
    snp_core = (jnp.dot(core_weights, core_geno, preferred_element_type=f32) / NSNP).astype(bf16)
    predicted = jnp.dot(snp_core, noncore_geno.T, preferred_element_type=f32)
    noncore_out = noncore_scale[None, :] * (noncore_vals - predicted)
    noncore_half = noncore_out.astype(bf16)
    snp_noncore = (jnp.dot(noncore_half, noncore_geno, preferred_element_type=f32) / NSNP).astype(bf16)
    back = jnp.dot(snp_noncore, core_geno.T, preferred_element_type=f32)
    core_rest = (core_vals.astype(f32) - back).astype(bf16)
    core_out = jnp.dot(core_rest, core_inv.T, preferred_element_type=f32)
    return noncore_out, core_out
```

```python
import functools

import jax
import jax.numpy as jnp
from jax import lax
from jax.sharding import PartitionSpec as P

F32, BF16 = jnp.float32, jnp.bfloat16
VALUE_CHUNKS = 2
MARKER_CHUNKS = 4


def contract_last(left, right):
    return lax.dot_general(
        left, right, (((1,), (1,)), ((), ())), preferred_element_type=F32
    )


def bits_of(count):
    return count.bit_length() - 1


def swap(x, axis, size, mask):
    return lax.ppermute(x, axis, [(i, i ^ mask) for i in range(size)])


def pick(x, index, axis=0):
    if isinstance(index, int):
        return lax.index_in_dim(x, index, axis, keepdims=False)
    return lax.dynamic_index_in_dim(x, index, axis, keepdims=False)


def add(x, y):
    return x.astype(F32) + y.astype(F32)


def bit_of(index, bit):
    return jnp.bitwise_and(jnp.right_shift(index, bit), 1)


def combine(items):
    return functools.reduce(jnp.add, [item.astype(F32) for item in items])


def reorder(items, index):
    for b in range(bits_of(len(items))):
        high = bit_of(index, b) == 1
        items = [jnp.where(high, items[i ^ (1 << b)], items[i]) for i in range(len(items))]
    return items


def scatter_snp(pieces, size):
    got = [swap(pieces[i], "snp", size, i) for i in reversed(range(1, size))]
    return combine([pieces[0]] + got)


def sum_snp(part, size, finish):
    s = lax.axis_index("snp")
    rows, cols = part.shape
    x = part.astype(BF16).reshape(size, rows // size, cols)
    mine = scatter_snp([pick(x, jnp.bitwise_xor(s, i)) for i in range(size)], size)
    mine = finish(mine).astype(BF16)
    items = [mine] + [swap(mine, "snp", size, i) for i in range(1, size)]
    return jnp.concatenate(reorder(items, s), axis=0)


def to_tile(part, na, ns, relative):
    a, s = lax.axis_index("anim"), lax.axis_index("snp")
    k = na // ns
    p = a // k
    x = part.reshape(ns, part.shape[0] // ns, part.shape[1])
    place = (lambda i: i) if relative else (lambda i: jnp.bitwise_xor(p, i))
    items = [pick(x, place(0))]
    items += [swap(pick(x, place(i)), "anim", na, i * k) for i in range(1, ns)]
    mine = scatter_snp(reorder(items, jnp.bitwise_xor(s, p)), ns).astype(BF16)
    rows = [None] * ns
    for i in reversed(range(1, ns)):
        rows[i] = swap(mine, "anim", na, i * k)
    rows[0] = mine
    blocks = [jnp.concatenate(rows, axis=0)]
    for b in range(bits_of(k)):
        high = bit_of(a, b) == 1
        other = [swap(block, "anim", na, 1 << b) for block in blocks]
        low = [jnp.where(high, o, m) for m, o in zip(blocks, other)]
        blocks = low + [jnp.where(high, m, o) for m, o in zip(blocks, other)]
    return blocks


def sum_anim(part, order, na, ns, finish):
    a = lax.axis_index("anim")
    nb, fixed = bits_of(na), bits_of(na // ns)
    rows, cols = part.shape
    x = part.astype(BF16).reshape([2] * nb + [rows // na, cols])
    axes = list(reversed(range(nb)))
    for n, b in enumerate(order):
        j = axes.index(b)
        bit = bit_of(a, b) if b < fixed else 0
        got = swap(pick(x, 1 - bit, j), "anim", na, 1 << b)
        x = add(pick(x, bit, j), got)
        if n < nb - 1:
            x = x.astype(BF16)
        axes.pop(j)
    x = finish(x).astype(BF16)
    for b in reversed(order):
        got = swap(x, "anim", na, 1 << b)
        axes = sorted(axes + [b], reverse=True)
        j = axes.index(b)
        if b < fixed:
            high = bit_of(a, b) == 1
            x = jnp.stack([jnp.where(high, got, x), jnp.where(high, x, got)], axis=j)
        else:
            x = jnp.stack([x, got], axis=j)
    return x.reshape(rows, cols)


def true_rows(x, na, ns):
    p = lax.axis_index("anim") // (na // ns)
    pieces = x.reshape(ns, x.shape[0] // ns, x.shape[1])
    return jnp.concatenate([pick(pieces, jnp.bitwise_xor(p, i)) for i in range(ns)], axis=0)


def local(na, ns, core_geno, noncore_geno, core_inv, snp_effects, noncore_scale):
    a = lax.axis_index("anim")
    reps, markers = snp_effects.shape
    total = markers * ns
    core_rows = core_geno.shape[0]
    vc = core_rows // VALUE_CHUNKS
    mc = markers // MARKER_CHUNKS
    nb = bits_of(na)
    orders = [[0] + list(range(1, nb)), [0] + list(reversed(range(1, nb)))]
    row_slices = [slice(i * vc, (i + 1) * vc) for i in range(VALUE_CHUNKS)]
    col_slices = [slice(i * mc, (i + 1) * mc) for i in range(MARKER_CHUNKS)]
    own_effects = pick(snp_effects.reshape(na, reps // na, markers), a)

    def tile_of(parts, relative):
        blocks = [to_tile(part.astype(BF16), na, ns, relative) for part in parts]
        return jnp.concatenate(
            [blocks[c][q] for q in range(na // ns) for c in range(VALUE_CHUNKS)], axis=1
        )

    def less(cols, x):
        return own_effects[:, cols].astype(F32) - x / total

    values = tile_of([contract_last(snp_effects, core_geno[rows]) for rows in row_slices], False)
    weights = jnp.concatenate(
        [sum_snp(contract_last(values, core_inv[rows]), ns, lambda x: x) for rows in row_slices],
        axis=1,
    )
    predicted = 0.0
    for n, cols in enumerate(col_slices):
        part = jnp.dot(weights, core_geno[:, cols], preferred_element_type=F32)
        rest = sum_anim(part, orders[n % 2], na, ns, functools.partial(less, cols))
        predicted = predicted + contract_last(rest, noncore_geno[:, cols])
    half = sum_snp(predicted, ns, lambda x: noncore_scale[None, :] * x)
    rests = []
    for n, cols in enumerate(col_slices):
        part = jnp.dot(half, noncore_geno[:, cols], preferred_element_type=F32)
        rests.append(sum_anim(part, orders[n % 2], na, ns, functools.partial(less, cols)))
    parts = []
    for rows in row_slices:
        terms = [contract_last(rest, core_geno[rows, cols]) for rest, cols in zip(rests, col_slices)]
        parts.append(functools.reduce(jnp.add, terms))
    core_rest = tile_of(parts, True)
    out = contract_last(core_rest, core_inv)
    core_out = scatter_snp(reorder(jnp.split(out.astype(BF16), ns, axis=1), lax.axis_index("snp")), ns)
    return true_rows(half, na, ns).astype(F32), true_rows(core_out, na, ns)


def solution(mesh):
    return jax.shard_map(
        functools.partial(local, mesh.shape["anim"], mesh.shape["snp"]),
        mesh=mesh,
        in_specs=(P("anim", "snp"), P("anim", "snp"), P("anim", "snp"), P(None, "snp"), P("anim")),
        out_specs=(P(None, "anim"), P(None, ("anim", "snp"))),
        check_vma=False,
    )
```

```python
import functools

import jax
import jax.numpy as jnp
from jax import lax
from jax.experimental import pallas as pl
from jax.experimental.pallas import tpu as pltpu
from jax.sharding import PartitionSpec as P

F32, BF16 = jnp.float32, jnp.bfloat16
VALUE_CHUNKS = 2
SNP_CORE_SHARES = (1, 1)


def contract_last(left, right):
    return lax.dot_general(
        left, right, (((1,), (1,)), ((), ())), preferred_element_type=F32
    )


def shares_of(count, shares):
    edges = [count * sum(shares[:i]) // sum(shares) for i in range(len(shares) + 1)]
    return [slice(low, high) for low, high in zip(edges, edges[1:])]


def halves_of(cols):
    middle = (cols.start + cols.stop) // 2
    return slice(cols.start, middle), slice(middle, cols.stop)


def after(x, earlier):
    return lax.optimization_barrier((x, earlier))[0]


def bits_of(count):
    return count.bit_length() - 1


def swap(x, axis, size, mask):
    return lax.ppermute(x, axis, [(i, i ^ mask) for i in range(size)])


def pick(x, index, axis=0):
    if isinstance(index, int):
        return lax.index_in_dim(x, index, axis, keepdims=False)
    return lax.dynamic_index_in_dim(x, index, axis, keepdims=False)


def add(x, y):
    return x.astype(F32) + y.astype(F32)


def bit_of(index, bit):
    return jnp.bitwise_and(jnp.right_shift(index, bit), 1)


def combine(items):
    return functools.reduce(jnp.add, [item.astype(F32) for item in items])


def reorder(items, index):
    for b in range(bits_of(len(items))):
        high = bit_of(index, b) == 1
        items = [jnp.where(high, items[i ^ (1 << b)], items[i]) for i in range(len(items))]
    return items


def scatter_snp(pieces, size):
    got = [swap(pieces[i], "snp", size, i) for i in reversed(range(1, size))]
    return combine([pieces[0]] + got)


def sum_snp(part, size, finish):
    s = lax.axis_index("snp")
    rows, cols = part.shape
    x = part.astype(BF16).reshape(size, rows // size, cols)
    mine = scatter_snp([pick(x, jnp.bitwise_xor(s, i)) for i in range(size)], size)
    mine = finish(mine).astype(BF16)
    items = [mine] + [swap(mine, "snp", size, i) for i in range(1, size)]
    return jnp.concatenate(reorder(items, s), axis=0)


def to_tile(part, na, ns, relative):
    a, s = lax.axis_index("anim"), lax.axis_index("snp")
    k = na // ns
    p = a // k
    x = part.reshape(ns, part.shape[0] // ns, part.shape[1])
    place = (lambda i: i) if relative else (lambda i: jnp.bitwise_xor(p, i))
    items = [pick(x, place(0))]
    items += [swap(pick(x, place(i)), "anim", na, i * k) for i in range(1, ns)]
    mine = scatter_snp(reorder(items, jnp.bitwise_xor(s, p)), ns).astype(BF16)
    rows = [None] * ns
    for i in reversed(range(1, ns)):
        rows[i] = swap(mine, "anim", na, i * k)
    rows[0] = mine
    blocks = [jnp.concatenate(rows, axis=0)]
    for b in range(bits_of(k)):
        high = bit_of(a, b) == 1
        other = [swap(block, "anim", na, 1 << b) for block in blocks]
        low = [jnp.where(high, o, m) for m, o in zip(blocks, other)]
        blocks = low + [jnp.where(high, m, o) for m, o in zip(blocks, other)]
    return blocks


class Order:
    def __init__(self):
        self.last = None

    def __call__(self, x):
        if self.last is not None:
            x = after(x, self.last)
        self.last = x
        return x


def sum_anim(order, make, na, ns, finish):
    a = lax.axis_index("anim")
    nb, fixed = bits_of(na), bits_of(na // ns)
    bit = bit_of(a, 0) if fixed else 0
    parts = make(order)
    rows, cols = parts[0].shape
    parts = [part.astype(BF16).reshape([2] * nb + [rows // na, cols]) for part in parts]
    send = order(jnp.concatenate([pick(x, 1 - bit, nb - 1) for x in parts], axis=-1))
    got = swap(send, "anim", na, 1)
    yield None
    got = order(got)
    halves = [
        add(pick(x, bit, nb - 1), got[..., i * cols : (i + 1) * cols]).astype(BF16)
        for i, x in enumerate(parts)
    ]
    routes = [list(range(1, nb)), list(reversed(range(1, nb)))]
    axes = [list(reversed(range(1, nb))) for _ in routes]
    for n in range(nb - 1):
        places = [axes[i].index(route[n]) for i, route in enumerate(routes)]
        sends = [order(pick(half, 1, j)) for half, j in zip(halves, places)]
        gots = [swap(send, "anim", na, 1 << route[n]) for send, route in zip(sends, routes)]
        yield None
        for i, j in enumerate(places):
            halves[i] = add(pick(halves[i], 0, j), order(gots[i]))
            if n < nb - 2:
                halves[i] = halves[i].astype(BF16)
            axes[i].pop(j)
    halves = [finish(i, half).astype(BF16) for i, half in enumerate(halves)]
    for n in reversed(range(nb - 1)):
        halves = [order(half) for half in halves]
        gots = [swap(half, "anim", na, 1 << route[n]) for half, route in zip(halves, routes)]
        yield None
        for i, route in enumerate(routes):
            axes[i] = sorted(axes[i] + [route[n]], reverse=True)
            j = axes[i].index(route[n])
            halves[i] = jnp.stack([halves[i], order(gots[i])], axis=j)
    x = order(jnp.concatenate(halves, axis=-1))
    got = swap(x, "anim", na, 1)
    yield None
    got = order(got)
    if fixed:
        odd = bit_of(a, 0) == 1
        x = jnp.stack([jnp.where(odd, got, x), jnp.where(odd, x, got)], axis=nb - 1)
    else:
        x = jnp.stack([x, got], axis=nb - 1)
    yield x.reshape(rows, 2 * cols)


def columns_of(tile, slices, earlier):
    def kernel(tile_ref, earlier_ref, *refs):
        outs, token_ref, sems = refs[: len(slices)], refs[-2], refs[-1]
        copies = [
            pltpu.make_async_copy(tile_ref.at[:, pl.ds(cols.start, cols.stop - cols.start)], out, sems.at[i])
            for i, (cols, out) in enumerate(zip(slices, outs))
        ]
        for copy in copies:
            copy.start()
        token_ref[...] = jnp.zeros_like(token_ref)
        for copy in copies:
            copy.wait()

    shape = lambda cols: jax.ShapeDtypeStruct((tile.shape[0], cols.stop - cols.start), tile.dtype)
    return pl.pallas_call(
        kernel,
        in_specs=[pl.BlockSpec(memory_space=pl.ANY)] * 2,
        out_specs=[pl.BlockSpec(memory_space=pl.ANY)] * len(slices)
        + [pl.BlockSpec(memory_space=pltpu.VMEM)],
        out_shape=[shape(cols) for cols in slices] + [jax.ShapeDtypeStruct((8, 128), F32)],
        scratch_shapes=[pltpu.SemaphoreType.DMA((len(slices),))],
        cost_estimate=pl.CostEstimate(
            flops=0, bytes_accessed=tile.size * tile.dtype.itemsize, transcendentals=0
        ),
        compiler_params=pltpu.CompilerParams(vmem_limit_bytes=30 << 20),
    )(tile, earlier)


def run_pair(makers, lead, na, ns, finishes, use, aside=None):
    order = Order()
    sums = [sum_anim(order, make, na, ns, finish) for make, finish in zip(makers, finishes)]
    uses = [None, None]

    def step(i):
        if uses[i] is not None:
            return next(uses[i], True)
        done = next(sums[i])
        if done is not None:
            uses[i] = use(order, i, done)
            return step(i)
        return False

    for _ in range(lead):
        step(0)
    count = 0
    while not step(1):
        step(0)
        count += 1
        if count == 2 and aside is not None:
            aside(order)
    while not step(0):
        pass


def true_rows(x, na, ns):
    p = lax.axis_index("anim") // (na // ns)
    pieces = x.reshape(ns, x.shape[0] // ns, x.shape[1])
    return jnp.concatenate([pick(pieces, jnp.bitwise_xor(p, i)) for i in range(ns)], axis=0)


def local(na, ns, core_geno, noncore_geno, core_inv, snp_effects, noncore_scale):
    a = lax.axis_index("anim")
    reps, markers = snp_effects.shape
    total = markers * ns
    core_rows = core_geno.shape[0]
    vc = core_rows // VALUE_CHUNKS
    row_slices = [slice(i * vc, (i + 1) * vc) for i in range(VALUE_CHUNKS)]
    own_effects = pick(snp_effects.reshape(na, reps // na, markers), a)

    def tile_of(parts, relative):
        blocks = [to_tile(part.astype(BF16), na, ns, relative) for part in parts]
        return jnp.concatenate(
            [blocks[c][q] for q in range(na // ns) for c in range(VALUE_CHUNKS)], axis=1
        )

    def less(cols, i, x):
        low = cols.start + i * x.shape[-1]
        return own_effects[:, low : low + x.shape[-1]].astype(F32) - x / total

    values = tile_of([contract_last(snp_effects, core_geno[rows]) for rows in row_slices], False)
    weights = jnp.concatenate(
        [sum_snp(contract_last(values, core_inv[rows]), ns, lambda x: x) for rows in row_slices],
        axis=1,
    )
    weights = lax.optimization_barrier(weights)
    weights = lax.optimization_barrier(weights)
    total_of = lambda items: functools.reduce(jnp.add, items)
    slices = shares_of(markers, SNP_CORE_SHARES)
    predicted = []

    def core_term(order, cols):
        left = weights if order.last is None else after(weights, order.last)
        return [
            jnp.dot(left, core_geno[:, mine], preferred_element_type=F32) for mine in halves_of(cols)
        ]

    noncore_slices = [mine for cols in slices for mine in halves_of(cols)]
    noncore_tiles = []

    def bring(order):
        *tiles, order.last = columns_of(noncore_geno, noncore_slices, order.last)
        noncore_tiles.extend(tiles)

    def use_core(order, n, rest):
        for i, low in enumerate(jnp.split(rest, 2, axis=1)):
            predicted.append(contract_last(low, noncore_tiles[2 * n + i]))
            if n == 0:
                predicted[-1] = order(predicted[-1])
        yield True

    run_pair(
        [functools.partial(core_term, cols=cols) for cols in slices],
        2, na, ns, [functools.partial(less, cols) for cols in slices], use_core, bring,
    )
    half = lax.optimization_barrier(
        sum_snp(total_of(predicted), ns, lambda x: noncore_scale[None, :] * x)
    )
    other = slices
    terms = [[] for _ in row_slices]

    def noncore_term(order, n):
        left = half if order.last is None else after(half, order.last)
        return [
            jnp.dot(left, tile, preferred_element_type=F32) for tile in noncore_tiles[2 * n : 2 * n + 2]
        ]

    def use_noncore(order, n, rest):
        for term, rows in zip(terms, row_slices):
            term.append(contract_last(rest, core_geno[rows, other[n]]))
            if n == 0:
                term[-1] = order(term[-1])
                yield False
        yield True

    run_pair(
        [functools.partial(noncore_term, n=n) for n in range(2)],
        2, na, ns, [functools.partial(less, cols) for cols in other], use_noncore,
    )
    parts = [total_of(term) for term in terms]
    core_rest = tile_of(parts, True)
    out = contract_last(core_rest, core_inv)
    core_out = scatter_snp(reorder(jnp.split(out.astype(BF16), ns, axis=1), lax.axis_index("snp")), ns)
    return true_rows(half, na, ns).astype(F32), true_rows(core_out, na, ns)


def solution(mesh):
    return jax.shard_map(
        functools.partial(local, mesh.shape["anim"], mesh.shape["snp"]),
        mesh=mesh,
        in_specs=(P("anim", "snp"), P("anim", "snp"), P("anim", "snp"), P(None, "snp"), P("anim")),
        out_specs=(P(None, "anim"), P(None, ("anim", "snp"))),
        check_vma=False,
    )
```

```python
import functools

import jax
import jax.numpy as jnp
from jax import lax
from jax.experimental import pallas as pl
from jax.experimental.pallas import tpu as pltpu
from jax.sharding import PartitionSpec as P

F32, BF16 = jnp.float32, jnp.bfloat16
VALUE_CHUNKS = 2
SNP_CORE_SHARES = (1, 1)


def contract_last(left, right):
    return lax.dot_general(
        left, right, (((1,), (1,)), ((), ())), preferred_element_type=F32
    )


def shares_of(count, shares):
    edges = [count * sum(shares[:i]) // sum(shares) for i in range(len(shares) + 1)]
    return [slice(low, high) for low, high in zip(edges, edges[1:])]


def halves_of(cols):
    middle = (cols.start + cols.stop) // 2
    return slice(cols.start, middle), slice(middle, cols.stop)


def after(x, earlier):
    return lax.optimization_barrier((x, earlier))[0]


def bits_of(count):
    return count.bit_length() - 1


def swap(x, axis, size, mask):
    return lax.ppermute(x, axis, [(i, i ^ mask) for i in range(size)])


def pick(x, index, axis=0):
    if isinstance(index, int):
        return lax.index_in_dim(x, index, axis, keepdims=False)
    return lax.dynamic_index_in_dim(x, index, axis, keepdims=False)


def add(x, y):
    return x.astype(F32) + y.astype(F32)


def bit_of(index, bit):
    return jnp.bitwise_and(jnp.right_shift(index, bit), 1)


def combine(items):
    return functools.reduce(jnp.add, [item.astype(F32) for item in items])


def reorder(items, index):
    for b in range(bits_of(len(items))):
        high = bit_of(index, b) == 1
        items = [jnp.where(high, items[i ^ (1 << b)], items[i]) for i in range(len(items))]
    return items


def scatter_snp(pieces, size):
    got = [swap(pieces[i], "snp", size, i) for i in reversed(range(1, size))]
    return combine([pieces[0]] + got)


def sum_snp(part, size, finish):
    s = lax.axis_index("snp")
    rows, cols = part.shape
    x = part.astype(BF16).reshape(size, rows // size, cols)
    mine = scatter_snp([pick(x, jnp.bitwise_xor(s, i)) for i in range(size)], size)
    mine = finish(mine).astype(BF16)
    items = [mine] + [swap(mine, "snp", size, i) for i in range(1, size)]
    return jnp.concatenate(reorder(items, s), axis=0)


def to_tile(part, na, ns, relative):
    a, s = lax.axis_index("anim"), lax.axis_index("snp")
    k = na // ns
    p = a // k
    x = part.reshape(ns, part.shape[0] // ns, part.shape[1])
    place = (lambda i: i) if relative else (lambda i: jnp.bitwise_xor(p, i))
    items = [pick(x, place(0))]
    items += [swap(pick(x, place(i)), "anim", na, i * k) for i in range(1, ns)]
    mine = scatter_snp(reorder(items, jnp.bitwise_xor(s, p)), ns).astype(BF16)
    rows = [None] * ns
    for i in reversed(range(1, ns)):
        rows[i] = swap(mine, "anim", na, i * k)
    rows[0] = mine
    blocks = [jnp.concatenate(rows, axis=0)]
    for b in range(bits_of(k)):
        high = bit_of(a, b) == 1
        other = [swap(block, "anim", na, 1 << b) for block in blocks]
        low = [jnp.where(high, o, m) for m, o in zip(blocks, other)]
        blocks = low + [jnp.where(high, m, o) for m, o in zip(blocks, other)]
    return blocks


class Order:
    def __init__(self):
        self.last = None

    def __call__(self, x):
        if self.last is not None:
            x = after(x, self.last)
        self.last = x
        return x


def sum_anim(order, make, na, ns, finish):
    a = lax.axis_index("anim")
    nb, fixed = bits_of(na), bits_of(na // ns)
    bit = bit_of(a, 0) if fixed else 0
    parts = make(order)
    rows, cols = parts[0].shape
    parts = [part.astype(BF16).reshape([2] * nb + [rows // na, cols]) for part in parts]
    send = order(jnp.concatenate([pick(x, 1 - bit, nb - 1) for x in parts], axis=-1))
    got = swap(send, "anim", na, 1)
    yield None
    got = order(got)
    halves = [
        add(pick(x, bit, nb - 1), got[..., i * cols : (i + 1) * cols]).astype(BF16)
        for i, x in enumerate(parts)
    ]
    routes = [list(range(1, nb)), list(reversed(range(1, nb)))]
    axes = [list(reversed(range(1, nb))) for _ in routes]
    for n in range(nb - 1):
        places = [axes[i].index(route[n]) for i, route in enumerate(routes)]
        sends = [order(pick(half, 1, j)) for half, j in zip(halves, places)]
        gots = [swap(send, "anim", na, 1 << route[n]) for send, route in zip(sends, routes)]
        yield None
        for i, j in enumerate(places):
            halves[i] = add(pick(halves[i], 0, j), order(gots[i]))
            if n < nb - 2:
                halves[i] = halves[i].astype(BF16)
            axes[i].pop(j)
    halves = [finish(i, half).astype(BF16) for i, half in enumerate(halves)]
    for n in reversed(range(nb - 1)):
        halves = [order(half) for half in halves]
        gots = [swap(half, "anim", na, 1 << route[n]) for half, route in zip(halves, routes)]
        yield None
        for i, route in enumerate(routes):
            axes[i] = sorted(axes[i] + [route[n]], reverse=True)
            j = axes[i].index(route[n])
            halves[i] = jnp.stack([halves[i], order(gots[i])], axis=j)
    x = order(jnp.concatenate(halves, axis=-1))
    got = swap(x, "anim", na, 1)
    yield None
    got = order(got)
    if fixed:
        odd = bit_of(a, 0) == 1
        x = jnp.stack([jnp.where(odd, got, x), jnp.where(odd, x, got)], axis=nb - 1)
    else:
        x = jnp.stack([x, got], axis=nb - 1)
    yield x.reshape(rows, 2 * cols)


def columns_of(tile, slices, earlier):
    def kernel(tile_ref, earlier_ref, *refs):
        outs, token_ref, sems = refs[: len(slices)], refs[-2], refs[-1]
        copies = [
            pltpu.make_async_copy(tile_ref.at[:, pl.ds(cols.start, cols.stop - cols.start)], out, sems.at[i])
            for i, (cols, out) in enumerate(zip(slices, outs))
        ]
        for copy in copies:
            copy.start()
        token_ref[...] = jnp.zeros_like(token_ref)
        for copy in copies:
            copy.wait()

    shape = lambda cols: jax.ShapeDtypeStruct((tile.shape[0], cols.stop - cols.start), tile.dtype)
    return pl.pallas_call(
        kernel,
        in_specs=[pl.BlockSpec(memory_space=pl.ANY)] * 2,
        out_specs=[pl.BlockSpec(memory_space=pl.ANY)] * len(slices)
        + [pl.BlockSpec(memory_space=pltpu.VMEM)],
        out_shape=[shape(cols) for cols in slices] + [jax.ShapeDtypeStruct((8, 128), F32)],
        scratch_shapes=[pltpu.SemaphoreType.DMA((len(slices),))],
        cost_estimate=pl.CostEstimate(
            flops=0, bytes_accessed=tile.size * tile.dtype.itemsize, transcendentals=0
        ),
        compiler_params=pltpu.CompilerParams(vmem_limit_bytes=30 << 20),
    )(tile, earlier)


def run_pair(makers, lead, na, ns, finishes, use, aside=None):
    order = Order()
    sums = [sum_anim(order, make, na, ns, finish) for make, finish in zip(makers, finishes)]
    uses = [None, None]

    def step(i):
        if uses[i] is not None:
            return next(uses[i], True)
        done = next(sums[i])
        if done is not None:
            uses[i] = use(order, i, done)
            return step(i)
        return False

    for _ in range(lead):
        step(0)
    count = 0
    while not step(1):
        step(0)
        count += 1
        if count == 2 and aside is not None:
            aside(order)
    while not step(0):
        pass


def true_rows(x, na, ns):
    p = lax.axis_index("anim") // (na // ns)
    pieces = x.reshape(ns, x.shape[0] // ns, x.shape[1])
    return jnp.concatenate([pick(pieces, jnp.bitwise_xor(p, i)) for i in range(ns)], axis=0)


def local(na, ns, core_geno, noncore_geno, core_inv, snp_effects, noncore_scale):
    a = lax.axis_index("anim")
    reps, markers = snp_effects.shape
    total = markers * ns
    core_rows = core_geno.shape[0]
    vc = core_rows // VALUE_CHUNKS
    row_slices = [slice(i * vc, (i + 1) * vc) for i in range(VALUE_CHUNKS)]
    own_effects = pick(snp_effects.reshape(na, reps // na, markers), a)

    def tile_of(parts, relative):
        blocks = [to_tile(part.astype(BF16), na, ns, relative) for part in parts]
        return jnp.concatenate(
            [blocks[c][q] for q in range(na // ns) for c in range(VALUE_CHUNKS)], axis=1
        )

    def less(cols, i, x):
        low = cols.start + i * x.shape[-1]
        return own_effects[:, low : low + x.shape[-1]].astype(F32) - x / total

    values = tile_of([contract_last(snp_effects, core_geno[rows]) for rows in row_slices], False)
    weights = jnp.concatenate(
        [sum_snp(contract_last(values, core_inv[rows]), ns, lambda x: x) for rows in row_slices],
        axis=1,
    )
    weights = lax.optimization_barrier(weights)
    weights = lax.optimization_barrier(weights)
    total_of = lambda items: functools.reduce(jnp.add, items)
    slices = shares_of(markers, SNP_CORE_SHARES)
    predicted = []

    def core_term(order, cols):
        left = weights if order.last is None else after(weights, order.last)
        if order.last is not None:
            part = jnp.dot(left, core_geno[:, cols], preferred_element_type=F32)
            return jnp.split(part.astype(BF16), 2, axis=1)
        return [
            jnp.dot(left, core_geno[:, mine], preferred_element_type=F32) for mine in halves_of(cols)
        ]

    noncore_slices = [mine for cols in slices for mine in halves_of(cols)]
    noncore_tiles = []

    def bring(order):
        *tiles, order.last = columns_of(noncore_geno, noncore_slices, order.last)
        noncore_tiles.extend(tiles)

    def use_core(order, n, rest):
        for i, low in enumerate(jnp.split(rest, 2, axis=1)):
            predicted.append(contract_last(low, noncore_tiles[2 * n + i]))
            if n == 0:
                predicted[-1] = order(predicted[-1])
        yield True

    run_pair(
        [functools.partial(core_term, cols=cols) for cols in slices],
        2, na, ns, [functools.partial(less, cols) for cols in slices], use_core, bring,
    )
    half = lax.optimization_barrier(
        sum_snp(total_of(predicted), ns, lambda x: noncore_scale[None, :] * x)
    )
    other = slices
    terms = [[] for _ in row_slices]

    def noncore_term(order, n):
        left = half if order.last is None else after(half, order.last)
        return [
            jnp.dot(left, tile, preferred_element_type=F32) for tile in noncore_tiles[2 * n : 2 * n + 2]
        ]

    def use_noncore(order, n, rest):
        if n == 0:
            whole = order(contract_last(rest, core_geno[:, other[0]]))
            for term, rows in zip(terms, row_slices):
                term.append(whole[:, rows])
        else:
            for term, rows in zip(terms, row_slices):
                term.append(contract_last(rest, core_geno[rows, other[1]]))
        yield True

    run_pair(
        [functools.partial(noncore_term, n=n) for n in range(2)],
        2, na, ns, [functools.partial(less, cols) for cols in other], use_noncore,
    )
    parts = [total_of(term) for term in terms]
    core_rest = tile_of(parts, True)
    out = contract_last(core_rest, core_inv)
    core_out = scatter_snp(reorder(jnp.split(out.astype(BF16), ns, axis=1), lax.axis_index("snp")), ns)
    return true_rows(half, na, ns).astype(F32), true_rows(core_out, na, ns)


def solution(mesh):
    return jax.shard_map(
        functools.partial(local, mesh.shape["anim"], mesh.shape["snp"]),
        mesh=mesh,
        in_specs=(P("anim", "snp"), P("anim", "snp"), P("anim", "snp"), P(None, "snp"), P("anim")),
        out_specs=(P(None, "anim"), P(None, ("anim", "snp"))),
        check_vma=False,
    )
```
